32 devices in a mesh: groups: 2 (over x), ctx: 16 (over z, y, core).
Axes of the slice: x: 2, y: 2, z: 4, core: 2. Of those that a mesh axis runs over, the one named last changes fastest.
Arguments:
- hidden: bfloat16 [4096, 16384], P(('groups', 'ctx')), parts along dimension 0, may hold values from -6 to 6
- norm_gain: float32 [16384], replicated, may hold values from 0.1 to 1.9
- w_key: bfloat16 [16384, 512], P('ctx'), may hold values from -0.046875 to 0.046875
- w_value: bfloat16 [16384, 512], P('ctx'), may hold values from -0.046875 to 0.046875
- query: bfloat16 [4096, 8192], P(('groups', 'ctx')), parts along dimension 0, may hold values from -256 to 256
- block_order: int32 [64], P('groups'), parts along dimension 0, may hold values from 0 to 31, each once
Outputs:
- attended: bfloat16 [4096, 8192], P(('groups', 'ctx')), parts along dimension 0
The draws below stay inside these ranges and needn't reach their ends.
There are 2 independent parts, one for each index of `groups`. The reference program is written for one: setup_inputs(seed, part) draws one part's arguments, and reference() takes and returns one part's arrays. A program takes and returns all parts, laid end to end along the dimension named above; an argument that names none is the same for every part. Nothing has to cross between parts.
Inputs may be any that keep to these rules, and one draw needn't show every extreme that they name: `block_order`: each number appears once.
All inputs are finite; a program needn't handle non-finite values.
Results may differ from the reference program's by a relative error of at most 0.0045.
The reference program's roundings to bfloat16 on the way count: a program that leaves them out, or rounds other values in their place, can miss the bound.
Values may be sent and summed in bfloat16 or wider, within the bound.
A program may use at most 128 MiB of HBM per device.

```python
import math
import jax
import jax.numpy as jnp
from jax import lax

D = 16384
QH = 64
KVH = 4
HD = 128
HALF = 64
TOKENS = 2048
BLOCKS = 32


def draw_query(key, part):
    key = jax.random.fold_in(key, 7)
    base_key = jax.random.fold_in(key, 0)
    query_shape = (TOKENS, QH, HD)
    query_draw = 2.5 * jax.random.normal(base_key, query_shape, jnp.float32)
    return jnp.clip(query_draw, -256.0, 256.0).reshape(TOKENS, QH * HD).astype(jnp.bfloat16)


def shard_levels(key, shape, cuts, low, largest):
    gain = 1.0
    for axis_at, shards_of in cuts:
        draws = jax.random.uniform(jax.random.fold_in(jax.random.fold_in(key, 6), axis_at), (shards_of,), jnp.float32, low / len(cuts), largest / len(cuts))
        gain = gain * jnp.repeat(jnp.exp(draws), shape[axis_at] // shards_of).reshape((-1,) + (1,) * (len(shape) - 1 - axis_at))
    return gain


def noise(stream_key, extent, deviation, limit, cuts=(), kind=jnp.bfloat16):
    entries = jax.random.normal(stream_key, extent, jnp.float32) * deviation
    if len(cuts) > 0:
        entries = shard_levels(stream_key, extent, cuts, -0.22, 0.18) * entries
    return jnp.clip(entries, min=-limit, max=limit).astype(kind)


def setup_inputs(seed: int = 0, part: int = 0) -> dict:
    key_list = jax.random.split(jax.random.key(seed), 7)
    part_keys = jax.random.split(jax.random.fold_in(key_list[6], part), 7)
    return {
        "hidden": noise(part_keys[0], (TOKENS, D), 1.0, 6.0, ((0, 16),)),
        "norm_gain": jnp.clip(1.0 + 0.18 * jax.random.normal(key_list[1], (D,), jnp.float32), 0.1, 1.9),
        "w_key": noise(key_list[2], (D, KVH * HD), D ** -0.5, 0.046875, ((0, 16),)),
        "w_value": noise(key_list[3], (D, KVH * HD), D ** -0.5, 0.046875, ((0, 16),)),
        "query": draw_query(jax.random.fold_in(jax.random.fold_in(key_list[6], part), 71), part),
        "block_order": jax.random.permutation(part_keys[5], BLOCKS).astype(jnp.int32),
    }


def rotate(raw_keys, positions):
    half_width = HD // 2
    freqs = jnp.exp(jnp.arange(half_width, dtype=jnp.float32) * (-2.0 * math.log(500000.0) / HD))
    angles = positions.astype(jnp.float32)[:, None] * freqs[None, :]
    cosine = jnp.cos(angles)[:, None, :]
    sine = jnp.sin(angles)[:, None, :]
    shaped = raw_keys.reshape(raw_keys.shape[0], -1, HD)
    front = shaped[..., :half_width]
    behind = shaped[..., half_width:]
    turned = jnp.concatenate([front * cosine - behind * sine, behind * cosine + front * sine], axis=-1)
    return turned.reshape(raw_keys.shape[0], -1)

def reference(hidden, norm_gain, w_key, w_value, query, block_order):
    row_ids = jnp.arange(TOKENS, dtype=jnp.int32)
    positions = block_order[row_ids // HALF] * HALF + row_ids % HALF
    widened = hidden.astype(jnp.float32)
    mean_square = lax.optimization_barrier(jnp.mean(widened * widened, axis=1, keepdims=True))
    normed = (widened * lax.rsqrt(mean_square + 1e-05) * norm_gain[None, :]).astype(jnp.bfloat16)
    keys = rotate(jnp.dot(normed, w_key, preferred_element_type=jnp.float32), positions).astype(jnp.bfloat16)
    values = jnp.dot(normed, w_value, preferred_element_type=jnp.float32).astype(jnp.bfloat16)
    group_size = QH // KVH
    queries = query.reshape(TOKENS, QH, HD).transpose(1, 0, 2)
    allowed = positions[None, :] <= positions[:, None]
    score_scale = 1.0 / math.sqrt(HD)

    def one_head(head):
        head_query = lax.dynamic_index_in_dim(queries, head, 0, keepdims=False)
        shared = (head // group_size).astype(jnp.int32) * HD
        head_keys = lax.dynamic_slice_in_dim(keys, shared, HD, 1)
        head_values = lax.dynamic_slice_in_dim(values, shared, HD, 1)
        scores = jnp.dot(head_query, head_keys.T, preferred_element_type=jnp.float32) * score_scale
        scores = jnp.where(allowed, scores, -1e+30)
        highest = lax.optimization_barrier(jnp.max(scores, axis=1, keepdims=True))
        weights = jnp.where(allowed, jnp.exp(scores - highest), 0.0)
        totals = lax.optimization_barrier(jnp.sum(weights, axis=1, keepdims=True))
        weighted = jnp.dot(weights.astype(jnp.bfloat16), head_values, preferred_element_type=jnp.float32)
        return (weighted / totals).astype(jnp.bfloat16)
    heads_out = lax.map(one_head, jnp.arange(QH, dtype=jnp.int32))
    return heads_out.transpose(1, 0, 2).reshape(TOKENS, QH * HD)
```

```python
import functools
import math

import jax
import jax.numpy as jnp
from jax import lax
from jax.experimental import pallas as pl
from jax.experimental.pallas import tpu as pltpu
from jax.sharding import PartitionSpec as P

HD = 128
MESH = pl.DeviceIdType.MESH


def project_kernel(
    G, Q, Z, hidden_ref, gain_ref, wk_ref, wv_ref, cos_ref, sin_ref, kv_ref,
    send_x, xs, wbuf, acc, pair_buf, part_buf,
    xs_send, xs_recv, w_send, w_recv, pair_send, pair_recv, part_send, part_recv,
    kv_send, kv_recv,
):
    rows, width = hidden_ref.shape
    feats = wk_ref.shape[0]
    fg = feats // G
    kw = wk_ref.shape[1]
    S = G * Q
    g = lax.axis_index("groups")
    c = lax.axis_index("ctx")
    z = c // Q
    i = c % Q
    me = g * Q + i
    right = lax.rem(z + 1, Z) * Q + i
    left = lax.rem(z + Z - 1, Z) * Q + i

    def plane(s):
        return (s // Q, z * Q + s % Q)

    barrier = pltpu.get_barrier_semaphore()
    for r in range(1, S):
        pl.semaphore_signal(barrier, inc=1, device_id=plane(lax.rem(me + r, S)), device_id_type=MESH)
    pl.semaphore_signal(barrier, inc=1, device_id=(g, right), device_id_type=MESH)
    pl.semaphore_signal(barrier, inc=1, device_id=(g, left), device_id_type=MESH)
    pl.semaphore_wait(barrier, S + 1)

    def weight_copy(step, j):
        origin = lax.rem(z + Z - step, Z)
        if step == 0:
            src = (wk_ref, wv_ref)[j].at[pl.ds(pl.multiple_of(g * fg, fg), fg)]
        else:
            src = wbuf.at[origin, j]
        return pltpu.make_async_remote_copy(
            src_ref=src, dst_ref=wbuf.at[origin, j],
            send_sem=w_send.at[step, j], recv_sem=w_recv.at[step, j],
            device_id=(g, right), device_id_type=MESH,
        )

    w_copies = [[weight_copy(step, j) for j in range(2)] for step in range(Z - 1)]
    for j in range(2):
        w_copies[0][j].start()

    piece = 1024
    def square(t, total):
        part = hidden_ref[:, pl.ds(pl.multiple_of(t * piece, piece), piece)].astype(jnp.float32)
        part = part * part
        out = total
        for u in range(piece // 128):
            out = out + part[:, u * 128:(u + 1) * 128]
        return out
    total = lax.fori_loop(0, width // piece, square, jnp.zeros((rows, 128), jnp.float32))
    scale = lax.rsqrt(jnp.sum(total, axis=1, keepdims=True) / width + 1e-05)

    def normalise(s, dst, row0):
        sg = s // Q
        si = s % Q
        def one(zo, carry):
            col = pl.multiple_of((zo * Q + si) * feats + sg * fg, 128)
            h = hidden_ref[:, pl.ds(col, fg)].astype(jnp.float32)
            n = h * scale * gain_ref[:, pl.ds(col, fg)]
            dst[pl.ds(row0, rows), pl.ds(pl.multiple_of(zo * fg, 128), fg)] = n.astype(jnp.bfloat16)
            return carry
        lax.fori_loop(0, Z, one, 0)

    order = [S - 1] if S == 1 else list(range(S - 1, 0, -1))
    x_copies = []
    for r in order:
        s = lax.rem(me + r, S)
        normalise(s, send_x, (r - 1) * rows)
        copy = pltpu.make_async_remote_copy(
            src_ref=send_x.at[pl.ds((r - 1) * rows, rows)],
            dst_ref=xs.at[pl.ds(pl.multiple_of(me * rows, rows), rows)],
            send_sem=xs_send.at[r - 1], recv_sem=xs_recv.at[r - 1],
            device_id=plane(s), device_id_type=MESH,
        )
        copy.start()
        x_copies.append(copy)
    normalise(me, xs, pl.multiple_of(me * rows, rows))
    for r, copy in zip(order, x_copies):
        src = lax.rem(me + S - r, S)
        slot = xs.at[pl.ds(pl.multiple_of(src * rows, rows), rows)]
        pltpu.make_async_remote_copy(
            src_ref=slot, dst_ref=slot, send_sem=xs_send.at[r - 1], recv_sem=xs_recv.at[r - 1],
            device_id=plane(src), device_id_type=MESH,
        ).wait_recv()

    tile = 256
    for step in range(Z):
        origin = lax.rem(z + Z - step, Z)
        if step > 0:
            for j in range(2):
                slot = wbuf.at[origin, j]
                pltpu.make_async_remote_copy(
                    src_ref=slot, dst_ref=slot, send_sem=w_send.at[step - 1, j],
                    recv_sem=w_recv.at[step - 1, j], device_id=(g, right), device_id_type=MESH,
                ).wait_recv()
                if step < Z - 1:
                    w_copies[step][j].start()
        for j in range(2):
            def one(t, carry, step=step, j=j, origin=origin):
                at = pl.ds(pl.multiple_of(t * tile, tile), tile)
                if step == 0:
                    weight = (wk_ref, wv_ref)[j][pl.ds(pl.multiple_of(g * fg, fg), fg), :]
                else:
                    weight = wbuf[origin, j]
                product = jnp.dot(
                    xs[at, pl.ds(pl.multiple_of(origin * fg, 128), fg)], weight,
                    preferred_element_type=jnp.float32,
                )
                cols = pl.ds(j * kw, kw)
                if step == 0:
                    acc[at, cols] = product
                else:
                    acc[at, cols] = acc[at, cols] + product
                return carry
            lax.fori_loop(0, S * rows // tile, one, 0)

    half = S // 2
    core = me % 2
    other = me + 1 - 2 * core
    chip = me // 2
    pair_copies = []
    for r in range(half):
        t = lax.rem(chip + 1 + r, half)
        copy = pltpu.make_async_remote_copy(
            src_ref=acc.at[pl.ds(pl.multiple_of((2 * t + 1 - core) * rows, rows), rows)],
            dst_ref=pair_buf.at[t],
            send_sem=pair_send.at[r], recv_sem=pair_recv.at[r],
            device_id=plane(other), device_id_type=MESH,
        )
        copy.start()
        pair_copies.append(copy)
    part_copies = []
    for r in range(half):
        t = lax.rem(chip + 1 + r, half)
        slot = pair_buf.at[t]
        pltpu.make_async_remote_copy(
            src_ref=slot, dst_ref=slot, send_sem=pair_send.at[r], recv_sem=pair_recv.at[r],
            device_id=plane(other), device_id_type=MESH,
        ).wait_recv()
        mine = pl.ds(pl.multiple_of((2 * t + core) * rows, rows), rows)
        pair_buf[t] = pair_buf[t] + acc[mine, :]
        if r < half - 1:
            copy = pltpu.make_async_remote_copy(
                src_ref=pair_buf.at[t], dst_ref=part_buf.at[r],
                send_sem=part_send.at[r], recv_sem=part_recv.at[r],
                device_id=plane(2 * t + core), device_id_type=MESH,
            )
            copy.start()
            part_copies.append(copy)
    raw = pair_buf[chip]
    for r in range(half - 1):
        part_copies[r].wait_recv()
        raw = raw + part_buf[r]

    cosine = cos_ref[...]
    sine = sin_ref[...]
    for h in range(kw // HD):
        u = raw[:, h * HD:(h + 1) * HD]
        swapped = pltpu.roll(u, HD // 2, 1)
        kv_ref[c, :, h * HD:(h + 1) * HD] = (u * cosine + swapped * sine).astype(jnp.bfloat16)
    kv_ref[c, :, kw:] = raw[:, kw:].astype(jnp.bfloat16)

    def hop(origin, device, stage, k):
        return pltpu.make_async_remote_copy(
            src_ref=kv_ref.at[origin], dst_ref=kv_ref.at[origin],
            send_sem=kv_send.at[stage, k], recv_sem=kv_recv.at[stage, k],
            device_id=(g, device), device_id_type=MESH,
        )

    bits = []
    bit = Q // 2
    while bit >= 1:
        bits.append(bit)
        bit //= 2

    def peer(bit):
        return c + bit - 2 * bit * ((i // bit) % 2)

    sent = []
    counts = [0] * (len(bits) + 1)

    def fan(origin, stage):
        for b in range(stage, len(bits)):
            k = counts[b + 1]
            counts[b + 1] += 1
            copy = hop(origin, peer(bits[b]), b + 1, k)
            copy.start()
            sent.append(copy)

    arrivals = {b: [] for b in range(len(bits))}
    for step in range(Z):
        origin = lax.rem(z + Z - step, Z) * Q + i
        if step > 0:
            hop(origin, right, 0, step - 1).wait_recv()
        if step < Z - 1:
            copy = hop(origin, right, 0, step)
            copy.start()
            sent.append(copy)
        fan(origin, 0)
    held = [lax.rem(z + Z - step, Z) * Q + i for step in range(Z)]
    for b, bit in enumerate(bits):
        flip = bit - 2 * bit * ((i // bit) % 2)
        fresh = []
        for k, origin in enumerate(held):
            came = origin + flip
            hop(came, peer(bit), b + 1, k).wait_recv()
            fan(came, b + 1)
            fresh.append(came)
        held = held + fresh

    for step in range(Z - 1):
        for j in range(2):
            w_copies[step][j].wait_send()
    for copy in x_copies + pair_copies + part_copies + sent:
        copy.wait_send()


def project(G, Q, Z, hidden, gain, w_key, w_value, cosine, sine):
    rows, width = hidden.shape
    feats, kw = w_key.shape
    S = G * Q
    n = Z * Q
    fg = feats // G
    half = S // 2
    nbits = Q.bit_length() - 1
    dma = pltpu.SemaphoreType.DMA
    vm = pl.BlockSpec(memory_space=pltpu.VMEM)
    return pl.pallas_call(
        functools.partial(project_kernel, G, Q, Z),
        out_shape=jax.ShapeDtypeStruct((n, rows, 2 * kw), jnp.bfloat16),
        in_specs=[vm] * 6,
        out_specs=vm,
        scratch_shapes=[
            pltpu.VMEM(((S - 1) * rows, Z * fg), jnp.bfloat16),
            pltpu.VMEM((S * rows, Z * fg), jnp.bfloat16),
            pltpu.VMEM((Z, 2, fg, kw), jnp.bfloat16),
            pltpu.VMEM((S * rows, 2 * kw), jnp.float32),
            pltpu.VMEM((half, rows, 2 * kw), jnp.float32),
            pltpu.VMEM((half - 1, rows, 2 * kw), jnp.float32),
            dma((S - 1,)), dma((S - 1,)),
            dma((Z - 1, 2)), dma((Z - 1, 2)),
            dma((half,)), dma((half,)),
            dma((half - 1,)), dma((half - 1,)),
            dma((nbits + 1, n)), dma((nbits + 1, n)),
        ],
        compiler_params=pltpu.CompilerParams(
            collective_id=0, has_side_effects=True, vmem_limit_bytes=52 * 1024 * 1024
        ),
        name="project",
    )(hidden, gain, w_key, w_value, cosine, sine)


def attend_kernel(heads, coeff, q_ref, k_ref, v_ref, bias_ref, out_ref, kt, eye):
    rows = q_ref.shape[0]

    @pl.when(pl.program_id(0) == 0)
    def _():
        kt[HD:, :] = bias_ref[...]
        a = lax.broadcasted_iota(jnp.int32, (rows, rows), 0)
        b = lax.broadcasted_iota(jnp.int32, (rows, rows), 1)
        eye[...] = jnp.where(a == b, 1.0, 0.0).astype(jnp.bfloat16)

    kt[:HD, :] = k_ref[...].T
    ident = eye[...]

    def pair(p):
        col = p * 2 * HD
        top = jnp.concatenate([q_ref[:, col:col + HD], ident], axis=1)
        low = jnp.concatenate([q_ref[:, col + HD:col + 2 * HD], ident], axis=1)
        q = jnp.concatenate([top, low], axis=0)
        s = jnp.dot(q, kt[...], preferred_element_type=jnp.float32)
        m = jnp.max(s, axis=1, keepdims=True) * coeff
        w = jnp.exp2(s * coeff - m)
        total = jnp.sum(w, axis=1, keepdims=True)
        o = jnp.dot(w.astype(jnp.bfloat16), v_ref[...], preferred_element_type=jnp.float32)
        o = (o / total).astype(jnp.bfloat16)
        out_ref[:, col:col + HD] = o[:rows]
        out_ref[:, col + HD:col + 2 * HD] = o[rows:]

    for p in range(heads // 2):
        pair(p)


def attend(query, kv, bias, kv_heads):
    rows, qw = query.shape
    keys = kv.shape[0]
    heads = qw // HD // kv_heads
    coeff = math.log2(math.e) / math.sqrt(HD)
    return pl.pallas_call(
        functools.partial(attend_kernel, heads, coeff),
        grid=(kv_heads,),
        out_shape=jax.ShapeDtypeStruct((rows, qw), jnp.bfloat16),
        in_specs=[
            pl.BlockSpec((rows, heads * HD), lambda h: (0, h)),
            pl.BlockSpec((keys, HD), lambda h: (0, h)),
            pl.BlockSpec((keys, HD), lambda h: (0, kv_heads + h)),
            pl.BlockSpec((rows, keys), lambda h: (0, 0)),
        ],
        out_specs=pl.BlockSpec((rows, heads * HD), lambda h: (0, h)),
        scratch_shapes=[
            pltpu.VMEM((HD + rows, keys), jnp.bfloat16),
            pltpu.VMEM((rows, rows), jnp.bfloat16),
        ],
        compiler_params=pltpu.CompilerParams(vmem_limit_bytes=52 * 1024 * 1024),
        name="attend",
    )(query, kv, kv, bias)


def body(G, Q, Z, hidden, norm_gain, w_key, w_value, query, block_order):
    rows = hidden.shape[0]
    half_rows = rows // 2
    kv_heads = w_key.shape[1] // HD
    device = lax.axis_index("ctx")
    local = jnp.arange(half_rows, dtype=jnp.int32)
    key_positions = (block_order[:, None] * half_rows + local[None, :]).reshape(-1)
    own = lax.dynamic_slice_in_dim(block_order, 2 * device, 2)
    positions = (own[:, None] * half_rows + local[None, :]).reshape(-1)
    freqs = jnp.exp(
        jnp.arange(HD // 2, dtype=jnp.float32) * (-2.0 * math.log(500000.0) / HD)
    )
    angles = positions.astype(jnp.float32)[:, None] * freqs[None, :]
    cosine = jnp.cos(angles)
    sine = jnp.sin(angles)
    kv = project(
        G, Q, Z, hidden, norm_gain[None, :], w_key, w_value,
        jnp.concatenate([cosine, cosine], axis=1), jnp.concatenate([-sine, sine], axis=1),
    )
    bias = jnp.where(key_positions[None, :] <= positions[:, None], 0.0, -1e30).astype(jnp.bfloat16)
    return attend(query, kv.reshape(-1, kv.shape[2]), bias, kv_heads)


def solution(mesh):
    G = mesh.shape["groups"]
    n = mesh.shape["ctx"]
    Q = 8 // G
    return jax.shard_map(
        functools.partial(body, G, Q, n // Q),
        mesh=mesh,
        in_specs=(
            P(("groups", "ctx"), None),
            P(),
            P("ctx", None),
            P("ctx", None),
            P(("groups", "ctx"), None),
            P("groups"),
        ),
        out_specs=P(("groups", "ctx"), None),
        check_vma=False,
    )
```

```python
import functools
import math

import jax
import jax.numpy as jnp
from jax import lax
from jax.experimental import pallas as pl
from jax.experimental.pallas import tpu as pltpu
from jax.sharding import PartitionSpec as P

HD = 128
MESH = pl.DeviceIdType.MESH


def project_kernel(
    G, Q, Z, hidden_ref, gain_ref, wk_ref, wv_ref, cos_ref, sin_ref, kv_ref,
    send_x, xs, wbuf, acc, pair_buf, part_buf,
    xs_send, xs_recv, w_send, w_recv, pair_send, pair_recv, part_send, part_recv,
    kv_send, kv_recv,
):
    rows, width = hidden_ref.shape
    feats = wk_ref.shape[0]
    fg = feats // G
    kw = wk_ref.shape[1]
    S = G * Q
    g = lax.axis_index("groups")
    c = lax.axis_index("ctx")
    z = c // Q
    i = c % Q
    me = g * Q + i
    right = lax.rem(z + 1, Z) * Q + i
    left = lax.rem(z + Z - 1, Z) * Q + i

    def plane(s):
        return (s // Q, z * Q + s % Q)

    barrier = pltpu.get_barrier_semaphore()
    for r in range(1, S):
        pl.semaphore_signal(barrier, inc=1, device_id=plane(lax.rem(me + r, S)), device_id_type=MESH)
    pl.semaphore_signal(barrier, inc=1, device_id=(g, right), device_id_type=MESH)
    pl.semaphore_signal(barrier, inc=1, device_id=(g, left), device_id_type=MESH)
    pl.semaphore_wait(barrier, S + 1)

    def weight_copy(step, j):
        origin = lax.rem(z + Z - step, Z)
        if step == 0:
            src = (wk_ref, wv_ref)[j].at[pl.ds(pl.multiple_of(g * fg, fg), fg)]
        else:
            src = wbuf.at[origin, j]
        return pltpu.make_async_remote_copy(
            src_ref=src, dst_ref=wbuf.at[origin, j],
            send_sem=w_send.at[step, j], recv_sem=w_recv.at[step, j],
            device_id=(g, right), device_id_type=MESH,
        )

    w_copies = [[weight_copy(step, j) for j in range(2)] for step in range(Z - 1)]
    for j in range(2):
        w_copies[0][j].start()

    piece = 1024
    def square(t, total):
        part = hidden_ref[:, pl.ds(pl.multiple_of(t * piece, piece), piece)].astype(jnp.float32)
        part = part * part
        out = total
        for u in range(piece // 128):
            out = out + part[:, u * 128:(u + 1) * 128]
        return out
    total = lax.fori_loop(0, width // piece, square, jnp.zeros((rows, 128), jnp.float32))
    scale = lax.rsqrt(jnp.sum(total, axis=1, keepdims=True) / width + 1e-05)

    def normalise(s, dst, row0):
        sg = s // Q
        si = s % Q
        def one(zo, carry):
            col = pl.multiple_of((zo * Q + si) * feats + sg * fg, 128)
            h = hidden_ref[:, pl.ds(col, fg)].astype(jnp.float32)
            n = h * scale * gain_ref[:, pl.ds(col, fg)]
            dst[pl.ds(row0, rows), pl.ds(pl.multiple_of(zo * fg, 128), fg)] = n.astype(jnp.bfloat16)
            return carry
        lax.fori_loop(0, Z, one, 0)

    order = [S - 1] if S == 1 else list(range(S - 1, 0, -1))
    x_copies = []
    for r in order:
        s = lax.rem(me + r, S)
        normalise(s, send_x, (r - 1) * rows)
        copy = pltpu.make_async_remote_copy(
            src_ref=send_x.at[pl.ds((r - 1) * rows, rows)],
            dst_ref=xs.at[pl.ds(pl.multiple_of(me * rows, rows), rows)],
            send_sem=xs_send.at[r - 1], recv_sem=xs_recv.at[r - 1],
            device_id=plane(s), device_id_type=MESH,
        )
        copy.start()
        x_copies.append(copy)
    normalise(me, xs, pl.multiple_of(me * rows, rows))

    def weight_arrives(step):
        origin = lax.rem(z + Z - step, Z)
        for j in range(2):
            slot = wbuf.at[origin, j]
            pltpu.make_async_remote_copy(
                src_ref=slot, dst_ref=slot, send_sem=w_send.at[step - 1, j],
                recv_sem=w_recv.at[step - 1, j], device_id=(g, right), device_id_type=MESH,
            ).wait_recv()
            if step < Z - 1:
                w_copies[step][j].start()

    for step in range(1, Z - 1):
        weight_arrives(step)
    for r, copy in zip(order, x_copies):
        src = lax.rem(me + S - r, S)
        slot = xs.at[pl.ds(pl.multiple_of(src * rows, rows), rows)]
        pltpu.make_async_remote_copy(
            src_ref=slot, dst_ref=slot, send_sem=xs_send.at[r - 1], recv_sem=xs_recv.at[r - 1],
            device_id=plane(src), device_id_type=MESH,
        ).wait_recv()

    tile = 256
    for step in range(Z):
        origin = lax.rem(z + Z - step, Z)
        if step == Z - 1:
            weight_arrives(step)
        for j in range(2):
            def one(t, carry, step=step, j=j, origin=origin):
                at = pl.ds(pl.multiple_of(t * tile, tile), tile)
                if step == 0:
                    weight = (wk_ref, wv_ref)[j][pl.ds(pl.multiple_of(g * fg, fg), fg), :]
                else:
                    weight = wbuf[origin, j]
                product = jnp.dot(
                    xs[at, pl.ds(pl.multiple_of(origin * fg, 128), fg)], weight,
                    preferred_element_type=jnp.float32,
                )
                cols = pl.ds(j * kw, kw)
                if step == 0:
                    acc[at, cols] = product
                else:
                    acc[at, cols] = acc[at, cols] + product
                return carry
            lax.fori_loop(0, S * rows // tile, one, 0)

    half = S // 2
    core = me % 2
    other = me + 1 - 2 * core
    chip = me // 2
    pair_copies = []
    for r in range(half):
        t = lax.rem(chip + 1 + r, half)
        copy = pltpu.make_async_remote_copy(
            src_ref=acc.at[pl.ds(pl.multiple_of((2 * t + 1 - core) * rows, rows), rows)],
            dst_ref=pair_buf.at[t],
            send_sem=pair_send.at[r], recv_sem=pair_recv.at[r],
            device_id=plane(other), device_id_type=MESH,
        )
        copy.start()
        pair_copies.append(copy)
    part_copies = []
    for r in range(half):
        t = lax.rem(chip + 1 + r, half)
        slot = pair_buf.at[t]
        pltpu.make_async_remote_copy(
            src_ref=slot, dst_ref=slot, send_sem=pair_send.at[r], recv_sem=pair_recv.at[r],
            device_id=plane(other), device_id_type=MESH,
        ).wait_recv()
        mine = pl.ds(pl.multiple_of((2 * t + core) * rows, rows), rows)
        pair_buf[t] = pair_buf[t] + acc[mine, :]
        if r < half - 1:
            copy = pltpu.make_async_remote_copy(
                src_ref=pair_buf.at[t], dst_ref=part_buf.at[r],
                send_sem=part_send.at[r], recv_sem=part_recv.at[r],
                device_id=plane(2 * t + core), device_id_type=MESH,
            )
            copy.start()
            part_copies.append(copy)
    raw = pair_buf[chip]
    for r in range(half - 1):
        part_copies[r].wait_recv()
        raw = raw + part_buf[r]

    cosine = cos_ref[...]
    sine = sin_ref[...]
    for h in range(kw // HD):
        u = raw[:, h * HD:(h + 1) * HD]
        swapped = pltpu.roll(u, HD // 2, 1)
        kv_ref[c, :, h * HD:(h + 1) * HD] = (u * cosine + swapped * sine).astype(jnp.bfloat16)
    kv_ref[c, :, kw:] = raw[:, kw:].astype(jnp.bfloat16)

    def hop(origin, device, stage, k):
        return pltpu.make_async_remote_copy(
            src_ref=kv_ref.at[origin], dst_ref=kv_ref.at[origin],
            send_sem=kv_send.at[stage, k], recv_sem=kv_recv.at[stage, k],
            device_id=(g, device), device_id_type=MESH,
        )

    bits = []
    bit = Q // 2
    while bit >= 1:
        bits.append(bit)
        bit //= 2

    def peer(bit):
        return c + bit - 2 * bit * ((i // bit) % 2)

    sent = []
    counts = [0] * (len(bits) + 1)

    def fan(origin, stage):
        for b in range(stage, len(bits)):
            k = counts[b + 1]
            counts[b + 1] += 1
            copy = hop(origin, peer(bits[b]), b + 1, k)
            copy.start()
            sent.append(copy)

    arrivals = {b: [] for b in range(len(bits))}
    for step in range(Z):
        origin = lax.rem(z + Z - step, Z) * Q + i
        if step > 0:
            hop(origin, right, 0, step - 1).wait_recv()
        if step < Z - 1:
            copy = hop(origin, right, 0, step)
            copy.start()
            sent.append(copy)
        fan(origin, 0)
    held = [lax.rem(z + Z - step, Z) * Q + i for step in range(Z)]
    for b, bit in enumerate(bits):
        flip = bit - 2 * bit * ((i // bit) % 2)
        fresh = []
        for k, origin in enumerate(held):
            came = origin + flip
            hop(came, peer(bit), b + 1, k).wait_recv()
            fan(came, b + 1)
            fresh.append(came)
        held = held + fresh

    for step in range(Z - 1):
        for j in range(2):
            w_copies[step][j].wait_send()
    for copy in x_copies + pair_copies + part_copies + sent:
        copy.wait_send()


def project(G, Q, Z, hidden, gain, w_key, w_value, cosine, sine):
    rows, width = hidden.shape
    feats, kw = w_key.shape
    S = G * Q
    n = Z * Q
    fg = feats // G
    half = S // 2
    nbits = Q.bit_length() - 1
    dma = pltpu.SemaphoreType.DMA
    vm = pl.BlockSpec(memory_space=pltpu.VMEM)
    return pl.pallas_call(
        functools.partial(project_kernel, G, Q, Z),
        out_shape=jax.ShapeDtypeStruct((n, rows, 2 * kw), jnp.bfloat16),
        in_specs=[vm] * 6,
        out_specs=vm,
        scratch_shapes=[
            pltpu.VMEM(((S - 1) * rows, Z * fg), jnp.bfloat16),
            pltpu.VMEM((S * rows, Z * fg), jnp.bfloat16),
            pltpu.VMEM((Z, 2, fg, kw), jnp.bfloat16),
            pltpu.VMEM((S * rows, 2 * kw), jnp.float32),
            pltpu.VMEM((half, rows, 2 * kw), jnp.float32),
            pltpu.VMEM((half - 1, rows, 2 * kw), jnp.float32),
            dma((S - 1,)), dma((S - 1,)),
            dma((Z - 1, 2)), dma((Z - 1, 2)),
            dma((half,)), dma((half,)),
            dma((half - 1,)), dma((half - 1,)),
            dma((nbits + 1, n)), dma((nbits + 1, n)),
        ],
        compiler_params=pltpu.CompilerParams(
            collective_id=0, has_side_effects=True, vmem_limit_bytes=52 * 1024 * 1024
        ),
        name="project",
    )(hidden, gain, w_key, w_value, cosine, sine)


def attend_kernel(heads, coeff, q_ref, k_ref, v_ref, bias_ref, out_ref, kt, eye):
    rows = q_ref.shape[0]

    @pl.when(pl.program_id(0) == 0)
    def _():
        kt[HD:, :] = bias_ref[...]
        a = lax.broadcasted_iota(jnp.int32, (rows, rows), 0)
        b = lax.broadcasted_iota(jnp.int32, (rows, rows), 1)
        eye[...] = jnp.where(a == b, 1.0, 0.0).astype(jnp.bfloat16)

    kt[:HD, :] = k_ref[...].T
    ident = eye[...]

    def pair(p):
        col = p * 2 * HD
        top = jnp.concatenate([q_ref[:, col:col + HD], ident], axis=1)
        low = jnp.concatenate([q_ref[:, col + HD:col + 2 * HD], ident], axis=1)
        q = jnp.concatenate([top, low], axis=0)
        s = jnp.dot(q, kt[...], preferred_element_type=jnp.float32)
        m = jnp.max(s, axis=1, keepdims=True) * coeff
        w = jnp.exp2(s * coeff - m)
        total = jnp.sum(w, axis=1, keepdims=True)
        o = jnp.dot(w.astype(jnp.bfloat16), v_ref[...], preferred_element_type=jnp.float32)
        o = (o / total).astype(jnp.bfloat16)
        out_ref[:, col:col + HD] = o[:rows]
        out_ref[:, col + HD:col + 2 * HD] = o[rows:]

    for p in range(heads // 2):
        pair(p)


def attend(query, kv, bias, kv_heads):
    rows, qw = query.shape
    keys = kv.shape[0]
    heads = qw // HD // kv_heads
    coeff = math.log2(math.e) / math.sqrt(HD)
    return pl.pallas_call(
        functools.partial(attend_kernel, heads, coeff),
        grid=(kv_heads,),
        out_shape=jax.ShapeDtypeStruct((rows, qw), jnp.bfloat16),
        in_specs=[
            pl.BlockSpec((rows, heads * HD), lambda h: (0, h)),
            pl.BlockSpec((keys, HD), lambda h: (0, h)),
            pl.BlockSpec((keys, HD), lambda h: (0, kv_heads + h)),
            pl.BlockSpec((rows, keys), lambda h: (0, 0)),
        ],
        out_specs=pl.BlockSpec((rows, heads * HD), lambda h: (0, h)),
        scratch_shapes=[
            pltpu.VMEM((HD + rows, keys), jnp.bfloat16),
            pltpu.VMEM((rows, rows), jnp.bfloat16),
        ],
        compiler_params=pltpu.CompilerParams(vmem_limit_bytes=52 * 1024 * 1024),
        name="attend",
    )(query, kv, kv, bias)


def body(G, Q, Z, hidden, norm_gain, w_key, w_value, query, block_order):
    rows = hidden.shape[0]
    half_rows = rows // 2
    kv_heads = w_key.shape[1] // HD
    device = lax.axis_index("ctx")
    local = jnp.arange(half_rows, dtype=jnp.int32)
    key_positions = (block_order[:, None] * half_rows + local[None, :]).reshape(-1)
    own = lax.dynamic_slice_in_dim(block_order, 2 * device, 2)
    positions = (own[:, None] * half_rows + local[None, :]).reshape(-1)
    freqs = jnp.exp(
        jnp.arange(HD // 2, dtype=jnp.float32) * (-2.0 * math.log(500000.0) / HD)
    )
    angles = positions.astype(jnp.float32)[:, None] * freqs[None, :]
    cosine = jnp.cos(angles)
    sine = jnp.sin(angles)
    kv = project(
        G, Q, Z, hidden, norm_gain[None, :], w_key, w_value,
        jnp.concatenate([cosine, cosine], axis=1), jnp.concatenate([-sine, sine], axis=1),
    )
    bias = jnp.where(key_positions[None, :] <= positions[:, None], 0.0, -1e30).astype(jnp.bfloat16)
    return attend(query, kv.reshape(-1, kv.shape[2]), bias, kv_heads)


def solution(mesh):
    G = mesh.shape["groups"]
    n = mesh.shape["ctx"]
    Q = 8 // G
    return jax.shard_map(
        functools.partial(body, G, Q, n // Q),
        mesh=mesh,
        in_specs=(
            P(("groups", "ctx"), None),
            P(),
            P("ctx", None),
            P("ctx", None),
            P(("groups", "ctx"), None),
            P("groups"),
        ),
        out_specs=P(("groups", "ctx"), None),
        check_vma=False,
    )
```
